32 devices in a mesh: groups: 2 (over x), dp: 16 (over z, y, core).
Axes of the slice: x: 2, y: 2, z: 4, core: 2. Of those that a mesh axis runs over, the one named last changes fastest.
Arguments:
- tokens: bfloat16 [16384, 4096], P(('groups', 'dp')), parts along dimension 0, may hold values from -6 to 6
- base_weight: bfloat16 [4096, 1024], P('dp'), may hold values from -0.09375 to 0.09375
- shrink_store: bfloat16 [32, 4096, 64], P('dp'), may hold values from -0.09375 to 0.09375
- expand_store: bfloat16 [32, 64, 1024], P('dp'), may hold values from -0.75 to 0.75
- request_adapter: int32 [64], P('groups'), parts along dimension 0, may hold values from 0 to 31
- adapter_slot: int32 [32], replicated, may hold values from 0 to 31, each once
Outputs:
- mixed: bfloat16 [16384, 1024], P(('groups', 'dp')), parts along dimension 0
The draws below stay inside these ranges and needn't reach their ends.
There are 2 independent parts, one for each index of `groups`. The reference program is written for one: setup_inputs(seed, part) draws one part's arguments, and reference() takes and returns one part's arrays. A program takes and returns all parts, laid end to end along the dimension named above; an argument that names none is the same for every part. Nothing has to cross between parts.
Inputs may be any that keep to these rules, and one draw needn't show every extreme that they name: `request_adapter`: each request names one of the 32 adapters; some adapters are named by many requests. `adapter_slot`: each store slot holds exactly one adapter.
All inputs are finite; a program needn't handle non-finite values.
Results may differ from the reference program's by a relative error of at most 0.0052.
Values may be sent and summed in bfloat16 or wider, within the bound.
A program may use at most 128 MiB of HBM per device.

```python
import math
import jax
import jax.numpy as jnp
import numpy as np
from jax import lax

D = 4096
KV = 1024
R = 64
SEG = 256
REQUESTS = 32
TOKENS = 8192
ADAPTERS = 32


def plant(drawn, key, low, top_value):
    extent = drawn.shape
    place = [jax.random.randint(jax.random.fold_in(key, axis), (), 0, extent[axis]) for axis in range(len(extent))]
    drawn = drawn.at[tuple(place)].set(low)
    longest = extent.index(max(extent))
    place[longest] = (place[longest] + 1) % extent[longest]
    return drawn.at[tuple(place)].set(top_value)


def levels(own_key, shape, cuts, smallest, top_value):
    gain = 1.0
    for position, parts in cuts:
        heights = jax.random.uniform(jax.random.fold_in(jax.random.fold_in(own_key, 6), position), (parts,), jnp.float32, smallest / len(cuts), top_value / len(cuts))
        gain = gain * jnp.repeat(jnp.exp(heights), shape[position] // parts).reshape((-1,) + (1,) * (len(shape) - 1 - position))
    return gain


def cumulative_ranks(number_of, lean):
    loads = [(1 << 20) // math.isqrt(grade ** lean) + 1 for grade in range(1, number_of + 1)]
    width = 1 + sum(loads) // (1 << 30)
    return np.cumsum(np.array([max(1, weight // width) for weight in loads]))


def skewed_ids(key, extent, count, lean):
    grid = cumulative_ranks(count, lean)
    ticket = jax.random.randint(jax.random.fold_in(key, 1), extent, 0, int(grid[count - 1]))
    grade = jnp.searchsorted(jnp.asarray(grid, jnp.int32), ticket, side="right")
    return jax.random.permutation(jax.random.fold_in(key, 2), count)[grade].astype(jnp.int32)


def bell_draw(stream_key, extent, spread, bound, cuts=(), dtype=jnp.bfloat16):
    level = levels(stream_key, extent, cuts, -0.22, 0.18) if cuts else 1.0
    values = jax.random.normal(stream_key, extent, jnp.float32) * spread * level
    return jnp.minimum(jnp.maximum(values, -bound), bound).astype(dtype)


def setup_inputs(seed: int = 0, part: int = 0) -> dict:
    seeds = jax.random.split(jax.random.key(seed), 7)
    own_keys = jax.random.split(jax.random.fold_in(seeds[6], part), 7)
    tokens = bell_draw(own_keys[0], (TOKENS, D), 1.0, 6.0, ((0, 16),))
    base_weight = bell_draw(seeds[1], (D, KV), D ** -0.5, 0.09375, ((0, 16),))
    shrink_store = bell_draw(seeds[2], (ADAPTERS, D, R), D ** -0.5, 0.09375, ((0, 16),))
    expand_store = bell_draw(seeds[3], (ADAPTERS, R, KV), R ** -0.5, 0.75, ((0, 16),))
    request_adapter = plant(skewed_ids(own_keys[4], (REQUESTS,), ADAPTERS, 2), jax.random.fold_in(own_keys[4], 3), 0, ADAPTERS - 1).astype(jnp.int32)
    adapter_slot = jax.random.permutation(seeds[5], ADAPTERS).astype(jnp.int32)
    return dict(tokens=tokens, base_weight=base_weight, shrink_store=shrink_store, expand_store=expand_store, request_adapter=request_adapter, adapter_slot=adapter_slot)


def reference(tokens, base_weight, shrink_store, expand_store, request_adapter, adapter_slot):
    request_slot = adapter_slot[request_adapter].astype(jnp.int32)
    base_out = jnp.dot(tokens, base_weight, preferred_element_type=jnp.float32)

    def one_request(packed):
        rows, slot_id = packed
        shrunk = jnp.dot(rows, shrink_store[slot_id], preferred_element_type=jnp.float32).astype(jnp.bfloat16)
        return jnp.dot(shrunk, expand_store[slot_id], preferred_element_type=jnp.float32).astype(jnp.bfloat16)

    low_rank = lax.map(one_request, (tokens.reshape(REQUESTS, SEG, D), request_slot))
    low_rank = low_rank.reshape(TOKENS, KV)
    return (base_out + low_rank.astype(jnp.float32)).astype(jnp.bfloat16)
```

```python
import jax
import jax.numpy as jnp
from jax import lax
from jax.sharding import PartitionSpec as P


def routed_by_collectives(tokens, base_weight, shrink_store, expand_store, request_adapter, adapter_slot):
    dp_count = lax.axis_size("dp")
    slots, width, rank = shrink_store.shape
    outs = expand_store.shape[2]
    requests = request_adapter.shape[0]
    own = requests // dp_count
    gathered = lax.all_gather(base_weight, "dp", axis=0, tiled=True)
    slot_ids = adapter_slot[request_adapter]
    shares = jnp.concatenate(
        [
            shrink_store.reshape(slots, dp_count, -1),
            expand_store.reshape(slots, dp_count, -1),
        ],
        axis=2,
    )
    held = lax.all_to_all(shares, "dp", split_axis=1, concat_axis=0, tiled=True)
    picked = jnp.take(held, slot_ids, axis=0)
    mine = lax.all_to_all(picked, "dp", split_axis=0, concat_axis=1, tiled=True)
    cut = width * rank // dp_count
    down = mine[:, :, :cut].reshape(own, width, rank)
    up = mine[:, :, cut:].reshape(own, rank, outs)
    grouped = tokens.reshape(own, -1, width)
    shrunk = jnp.einsum("qsd,qdr->qsr", grouped, down, preferred_element_type=jnp.float32).astype(jnp.bfloat16)
    low_rank = jnp.einsum("qsr,qrc->qsc", shrunk, up, preferred_element_type=jnp.float32).astype(jnp.bfloat16)
    base_out = jnp.dot(tokens, gathered, preferred_element_type=jnp.float32)
    low_rank = low_rank.reshape(base_out.shape)
    return (base_out + low_rank.astype(jnp.float32)).astype(jnp.bfloat16)


def solution(mesh):
    return jax.shard_map(
        routed_by_collectives,
        mesh=mesh,
        in_specs=(
            P(("groups", "dp"), None),
            P("dp", None),
            P("dp", None, None),
            P("dp", None, None),
            P("groups"),
            P(),
        ),
        out_specs=P(("groups", "dp"), None),
        check_vma=False,
    )
```

```python
import jax
import jax.numpy as jnp
from jax import lax
from jax.experimental import pallas as pl
from jax.experimental.pallas import tpu as pltpu
from jax.sharding import PartitionSpec as P

MESH = pl.DeviceIdType.MESH
LANES = 128
TILE = 16
LAYERS = 4
CORE0, Z, Y, X, DY, DX, DX0, CZ, CY, CX, CD = 0, 0, 4, 7, 10, 13, 17, 17, 21, 24, 28
MESSAGES = 32


def prefill_kernel(
    request_ref, adapter_slot, tok_hbm, w_hbm, shrink, expand, out_ref,
    weight, tok, total, shares, held, picks, mine, ids_in, ids,
    local_sem, base_send, base_recv, one_send, one_recv, two_send, two_recv, ids_send, ids_recv,
):
    gx, dp = lax.axis_index("groups"), lax.axis_index("dp")
    groups, dp_count = lax.axis_size("groups"), lax.axis_size("dp")
    devices = groups * dp_count
    me = gx * dp_count + dp
    core = dp % 2
    y = (dp // 2) % 2
    z = dp // 4
    shard = w_hbm.shape[0]
    piece = shard // 2
    half = piece // 2
    width = tok_hbm.shape[1]
    deep = width // 2 // devices
    own = mine.shape[0]
    layers = [z, z + 1 - 2 * (z % 2), (z + 2) % LAYERS, LAYERS - 1 - z]

    barrier = pltpu.get_barrier_semaphore()

    def greet(i, _):
        other = (me + i) % devices
        pl.semaphore_signal(
            barrier, inc=1, device_id=(other // dp_count, other % dp_count), device_id_type=MESH
        )
        return 0

    lax.fori_loop(1, devices, greet, 0)
    load_tok = pltpu.make_async_copy(tok_hbm, tok, local_sem.at[0])
    load_tok.start()
    load_w = pltpu.make_async_copy(
        w_hbm, weight.at[pl.ds(pl.multiple_of(dp * shard, shard), shard)], local_sem.at[1]
    )
    load_w.start()

    share_first = gx * dp_count

    def pack(i, _):
        k = share_first + i
        low = pl.multiple_of(k * deep, TILE)
        high = pl.multiple_of(width // 2 + k * deep, TILE)
        row = pl.multiple_of((k // 8) * TILE, TILE)
        col = pl.multiple_of((k % 8) * LANES, LANES)
        for s in range(shrink.shape[0]):
            shares[i, s, :deep, :] = jnp.concatenate(
                [shrink[s, pl.ds(low, deep), :], shrink[s, pl.ds(high, deep), :]], axis=1
            )
            shares[i, s, deep:, :] = expand[s, pl.ds(row, TILE), pl.ds(col, LANES)]
        return 0

    lax.fori_loop(0, dp_count, pack, 0)
    pl.semaphore_wait(barrier, devices - 1)

    def rows_of(layer, of_x, of_y, first=0, count=piece):
        owner = (layer * 2 + of_y) * 2 + core
        return pl.ds(pl.multiple_of(owner * shard + of_x * piece + first, TILE), count)

    def rows_of_other(layer, of_x, of_y, count=piece):
        owner = (layer * 2 + of_y) * 2 + 1 - core
        return pl.ds(pl.multiple_of(owner * shard + of_x * piece, TILE), count)

    def message(number, src, rows, target):
        return pltpu.make_async_remote_copy(
            src_ref=src, dst_ref=weight.at[rows],
            send_sem=base_send.at[number], recv_sem=base_recv.at[number],
            device_id=target, device_id_type=MESH,
        )

    sent = []

    def send(number, rows, target, src=None):
        copy = message(number, weight.at[rows] if src is None else src, rows, target)
        copy.start()
        sent.append(copy)

    def landed(number, rows):
        message(number, weight.at[rows], rows, other_core).wait_recv()

    fx, fy = 1 - gx, 1 - y
    other_core = (gx, dp + 1 - 2 * core)
    x_peer = (fx, dp)
    y_peer = (gx, dp + 2 - 4 * y)
    own_piece = w_hbm.at[pl.ds(pl.multiple_of(gx * piece, TILE), piece)]

    swap_ids = pltpu.make_async_remote_copy(
        src_ref=request_ref, dst_ref=ids_in, send_sem=ids_send, recv_sem=ids_recv,
        device_id=x_peer, device_id_type=MESH,
    )
    swap_ids.start()
    for i in range(1, LAYERS):
        send(Z + i, rows_of(z, gx, y), (gx, (layers[i] * 2 + y) * 2 + core), own_piece)
    send(Y, rows_of(z, gx, y), y_peer, own_piece)
    send(CORE0, rows_of(z, 0, y, count=shard), other_core, w_hbm)

    def share_copy(i, to, owner):
        return pltpu.make_async_remote_copy(
            src_ref=shares.at[to], dst_ref=held.at[pl.ds(owner * shrink.shape[0], shrink.shape[0])],
            send_sem=one_send.at[i], recv_sem=one_recv.at[i],
            device_id=(gx, to), device_id_type=MESH,
        )

    def send_share(i, _):
        share_copy(i, (dp + i) % dp_count, dp).start()
        return 0

    lax.fori_loop(1, dp_count, send_share, 0)
    held[pl.ds(dp * shrink.shape[0], shrink.shape[0])] = shares[dp]

    own_ids = pltpu.make_async_copy(request_ref, ids.at[gx], local_sem.at[2])
    own_ids.start()
    swap_ids.wait_recv()
    their_ids = pltpu.make_async_copy(ids_in, ids.at[fx], local_sem.at[3])
    their_ids.start()
    own_ids.wait()
    their_ids.wait()

    landed(Y, rows_of(z, gx, fy))
    send(DX0, rows_of(z, gx, fy), x_peer)
    send(CY, rows_of(z, gx, fy), other_core)
    for i in range(1, LAYERS):
        rows = rows_of(layers[i], gx, y)
        landed(Z + i, rows)
        send(Y + i, rows, y_peer)
        send(X + i, rows, x_peer)
        send(CZ + i, rows, other_core)

    def wait_share(i, _):
        share_copy(i, dp, (dp + dp_count - i) % dp_count).wait_recv()
        return 0

    lax.fori_loop(1, dp_count, wait_share, 0)

    def pick_copy(i, to, holder):
        return pltpu.make_async_remote_copy(
            src_ref=picks.at[to], dst_ref=mine.at[:, holder],
            send_sem=two_send.at[i], recv_sem=two_recv.at[i],
            device_id=(to // dp_count, to % dp_count), device_id_type=MESH,
        )

    def pick(to, j):
        return held[adapter_slot[ids[to // dp_count, 0, (to % dp_count) * own + j]]]

    def send_pick(i, _):
        to = (me + i) % devices
        for j in range(own):
            picks[to, j] = pick(to, j)
        pick_copy(i, to, me).start()
        return 0

    lax.fori_loop(1, devices, send_pick, 0)
    for j in range(own):
        mine[j, me] = pick(me, j)

    for i in range(1, LAYERS):
        rows = rows_of(layers[i], fx, y)
        landed(X + i, rows)
        send(DY + i, rows_of(layers[i], fx, y, 0, half), y_peer)
        send(CX + i, rows, other_core)
        rows = rows_of(layers[i], gx, fy)
        landed(Y + i, rows)
        send(DX + i, rows_of(layers[i], gx, fy, half, half), x_peer)
        send(CY + i, rows, other_core)
    rows = rows_of(z, fx, fy)
    landed(DX0, rows)
    send(CD, rows, other_core)
    for i in range(1, LAYERS):
        landed(DY + i, rows_of(layers[i], fx, fy, 0, half))
        landed(DX + i, rows_of(layers[i], fx, fy, half, half))
        send(CD + i, rows_of(layers[i], fx, fy), other_core)

    load_tok.wait()
    load_w.wait()
    block = 4 * shard
    column = 256
    for i in range(LAYERS):
        layer = layers[i]
        if i == 0:
            landed(CORE0, rows_of_other(z, 0, y, count=shard))
        else:
            landed(CZ + i, rows_of_other(layer, gx, y))
            landed(CX + i, rows_of_other(layer, fx, y))
        landed(CY + i, rows_of_other(layer, gx, fy))
        landed(CD + i, rows_of_other(layer, fx, fy))
        place = pl.ds(pl.multiple_of(layer * block, block), block)

        def add(n, _):
            cols = pl.ds(pl.multiple_of(n * column, column), column)
            term = jnp.dot(tok[:, place], weight[place, cols], preferred_element_type=jnp.float32)
            total[:, cols] = term if i == 0 else total[:, cols] + term
            return 0

        lax.fori_loop(0, total.shape[1] // column, add, 0)

    def wait_pick(i, _):
        pick_copy(i, me, (me + devices - i) % devices).wait_recv()
        return 0

    lax.fori_loop(1, devices, wait_pick, 0)
    seg = tok.shape[0] // own
    rank = shrink.shape[2]
    for j in range(own):
        lines = pl.ds(j * seg, seg)
        down = mine[j, :, :deep, :].reshape(width // 2, LANES)
        first = jnp.dot(tok[lines, : width // 2], down, preferred_element_type=jnp.float32)
        second = jnp.dot(tok[lines, width // 2 :], down, preferred_element_type=jnp.float32)
        shrunk = (first + pltpu.roll(second, rank, 1))[:, :rank].astype(jnp.bfloat16)
        up = jnp.concatenate(
            [
                jnp.concatenate([mine[j, r * 8 + c, deep:, :] for c in range(8)], axis=1)
                for r in range(rank // TILE)
            ],
            axis=0,
        )
        low_rank = jnp.dot(shrunk, up, preferred_element_type=jnp.float32).astype(jnp.bfloat16)
        out_ref[lines, :] = (total[lines, :] + low_rank.astype(jnp.float32)).astype(out_ref.dtype)

    for copy in sent:
        copy.wait_send()
    swap_ids.wait_send()

    def drain_one(i, _):
        share_copy(i, (dp + i) % dp_count, dp).wait_send()
        return 0

    def drain_two(i, _):
        pick_copy(i, (me + i) % devices, me).wait_send()
        return 0

    lax.fori_loop(1, dp_count, drain_one, 0)
    lax.fori_loop(1, devices, drain_two, 0)


def in_one_kernel(tokens, base_weight, shrink_store, expand_store, request_adapter, adapter_slot):
    groups, dp_count = lax.axis_size("groups"), lax.axis_size("dp")
    devices = groups * dp_count
    rows, width = tokens.shape
    slots, _, rank = shrink_store.shape
    outs = base_weight.shape[1]
    requests = request_adapter.shape[0]
    own = requests // dp_count
    tall = width // 2 // devices + TILE
    bf16 = jnp.bfloat16
    vmem = pl.BlockSpec(memory_space=pltpu.VMEM)
    anywhere = pl.BlockSpec(memory_space=pl.ANY)
    dma = pltpu.SemaphoreType.DMA
    return pl.pallas_call(
        prefill_kernel,
        out_shape=jax.ShapeDtypeStruct((rows, outs), bf16),
        in_specs=[vmem, pl.BlockSpec(memory_space=pltpu.SMEM), anywhere, anywhere, vmem, vmem],
        out_specs=vmem,
        scratch_shapes=[
            pltpu.VMEM((width, outs), bf16),
            pltpu.VMEM((rows, width), bf16),
            pltpu.VMEM((rows, outs), jnp.float32),
            pltpu.VMEM((dp_count, slots, tall, LANES), bf16),
            pltpu.VMEM((dp_count * slots, tall, LANES), bf16),
            pltpu.VMEM((devices, own, tall, LANES), bf16),
            pltpu.VMEM((own, devices, tall, LANES), bf16),
            pltpu.VMEM((1, requests), jnp.int32),
            pltpu.SMEM((groups, 1, requests), jnp.int32),
            dma((4,)),
            dma((MESSAGES,)),
            dma((MESSAGES,)),
            dma((dp_count,)),
            dma((dp_count,)),
            dma((devices,)),
            dma((devices,)),
            dma,
            dma,
        ],
        compiler_params=pltpu.CompilerParams(
            collective_id=0, has_side_effects=True, vmem_limit_bytes=56 * 1024 * 1024
        ),
        cost_estimate=pl.CostEstimate(
            flops=2 * rows * width * (outs + 2 * rank), bytes_accessed=16 * 1024 * 1024, transcendentals=0
        ),
    )(request_adapter.reshape(1, requests), adapter_slot, tokens, base_weight, shrink_store, expand_store)


def routed_by_collectives(tokens, base_weight, shrink_store, expand_store, request_adapter, adapter_slot):
    dp_count = lax.axis_size("dp")
    slots, width, rank = shrink_store.shape
    outs = expand_store.shape[2]
    requests = request_adapter.shape[0]
    own = requests // dp_count
    gathered = lax.all_gather(base_weight, "dp", axis=0, tiled=True)
    slot_ids = adapter_slot[request_adapter]
    shares = jnp.concatenate(
        [
            shrink_store.reshape(slots, dp_count, -1),
            expand_store.reshape(slots, dp_count, -1),
        ],
        axis=2,
    )
    held = lax.all_to_all(shares, "dp", split_axis=1, concat_axis=0, tiled=True)
    picked = jnp.take(held, slot_ids, axis=0)
    mine = lax.all_to_all(picked, "dp", split_axis=0, concat_axis=1, tiled=True)
    cut = width * rank // dp_count
    down = mine[:, :, :cut].reshape(own, width, rank)
    up = mine[:, :, cut:].reshape(own, rank, outs)
    grouped = tokens.reshape(own, -1, width)
    shrunk = jnp.einsum("qsd,qdr->qsr", grouped, down, preferred_element_type=jnp.float32).astype(jnp.bfloat16)
    low_rank = jnp.einsum("qsr,qrc->qsc", shrunk, up, preferred_element_type=jnp.float32).astype(jnp.bfloat16)
    base_out = jnp.dot(tokens, gathered, preferred_element_type=jnp.float32)
    low_rank = low_rank.reshape(base_out.shape)
    return (base_out + low_rank.astype(jnp.float32)).astype(jnp.bfloat16)


def solution(mesh):
    square = mesh.shape["groups"] == 2 and mesh.shape["dp"] == 16
    return jax.shard_map(
        in_one_kernel if square else routed_by_collectives,
        mesh=mesh,
        in_specs=(
            P(("groups", "dp"), None),
            P("dp", None),
            P("dp", None, None),
            P("dp", None, None),
            P("groups"),
            P(),
        ),
        out_specs=P(("groups", "dp"), None),
        check_vma=False,
    )
```

```python
import jax
import jax.numpy as jnp
from jax import lax
from jax.experimental import pallas as pl
from jax.experimental.pallas import tpu as pltpu
from jax.sharding import PartitionSpec as P

MESH = pl.DeviceIdType.MESH
LANES = 128
TILE = 16
LAYERS = 4
CORE0, Z, Y, X, DY, DX, DX0, CZ, CY, CX, CD = 0, 0, 4, 7, 10, 13, 17, 17, 21, 24, 28
MESSAGES = 32
RELAY = 32
SENDS = 36


def prefill_kernel(
    request_ref, adapter_slot, tok_hbm, w_hbm, shrink, expand, out_ref,
    weight, tok, total, shares, held, picks, mine, ids_in, ids,
    local_sem, base_send, base_recv, one_send, one_recv, two_send, two_recv, ids_send, ids_recv,
):
    gx, dp = lax.axis_index("groups"), lax.axis_index("dp")
    groups, dp_count = lax.axis_size("groups"), lax.axis_size("dp")
    devices = groups * dp_count
    me = gx * dp_count + dp
    core = dp % 2
    y = (dp // 2) % 2
    z = dp // 4
    shard = w_hbm.shape[0]
    piece = shard // 2
    half = piece // 2
    width = tok_hbm.shape[1]
    rank = shrink.shape[1]
    own = mine.shape[0]
    side = z // 2
    inner = ((z + 1) // 2) % 2
    near, across = z + 1 - 2 * (z % 2), LAYERS - 1 - z
    layers = [z, near, 2 - side, 3 - 3 * side]

    barrier = pltpu.get_barrier_semaphore()

    def greet(i, _):
        other = (me + i) % devices
        pl.semaphore_signal(
            barrier, inc=1, device_id=(other // dp_count, other % dp_count), device_id_type=MESH
        )
        return 0

    lax.fori_loop(1, devices, greet, 0)
    load_tok = pltpu.make_async_copy(tok_hbm, tok, local_sem.at[0])
    load_tok.start()
    load_w = pltpu.make_async_copy(
        w_hbm, weight.at[pl.ds(pl.multiple_of(dp * shard, shard), shard)], local_sem.at[1]
    )
    load_w.start()

    share_first = gx * dp_count

    def pack(i, _):
        k = share_first + i
        col = pl.multiple_of(k * LANES, LANES)
        up_row = pl.multiple_of((k // 8) * TILE, TILE)
        up_col = pl.multiple_of((k % 8) * LANES, LANES)
        for s in range(shrink.shape[0]):
            shares[i, s, :rank, :] = shrink[s, :, pl.ds(col, LANES)]
            shares[i, s, rank:, :] = expand[s, pl.ds(up_row, TILE), pl.ds(up_col, LANES)]
        return 0

    lax.fori_loop(0, dp_count, pack, 0)
    pl.semaphore_wait(barrier, devices - 1)

    def rows_of(layer, of_x, of_y, first=0, count=piece):
        owner = (layer * 2 + of_y) * 2 + core
        return pl.ds(pl.multiple_of(owner * shard + of_x * piece + first, TILE), count)

    def rows_of_other(layer, of_x, of_y, count=piece):
        owner = (layer * 2 + of_y) * 2 + 1 - core
        return pl.ds(pl.multiple_of(owner * shard + of_x * piece, TILE), count)

    def message(number, src, rows, target, send_number=None):
        return pltpu.make_async_remote_copy(
            src_ref=src, dst_ref=weight.at[rows],
            send_sem=base_send.at[number if send_number is None else send_number], recv_sem=base_recv.at[number],
            device_id=target, device_id_type=MESH,
        )

    sent = []

    def send(number, rows, target, src=None):
        copy = message(number, weight.at[rows] if src is None else src, rows, target)
        copy.start()
        sent.append(copy)

    def landed(number, rows):
        message(number, weight.at[rows], rows, other_core).wait_recv()

    fx, fy = 1 - gx, 1 - y
    other_core = (gx, dp + 1 - 2 * core)
    x_peer = (fx, dp)
    y_peer = (gx, dp + 2 - 4 * y)
    own_piece = w_hbm.at[pl.ds(pl.multiple_of(gx * piece, TILE), piece)]

    swap_ids = pltpu.make_async_remote_copy(
        src_ref=request_ref, dst_ref=ids_in, send_sem=ids_send, recv_sem=ids_recv,
        device_id=x_peer, device_id_type=MESH,
    )
    swap_ids.start()
    near_peer = (gx, (near * 2 + y) * 2 + core)
    across_peer = (gx, (across * 2 + y) * 2 + core)
    relays = []

    def relay(number, rows, target, send_number, src=None):
        copy = message(number, weight.at[rows] if src is None else src, rows, target, send_number)
        relays.append(copy)

        @pl.when(inner == 1)
        def _():
            copy.start()

    def share_copy(i, to, owner):
        return pltpu.make_async_remote_copy(
            src_ref=shares.at[to], dst_ref=held.at[pl.ds(owner * shrink.shape[0], shrink.shape[0])],
            send_sem=one_send.at[i], recv_sem=one_recv.at[i],
            device_id=(gx, to), device_id_type=MESH,
        )

    def send_share(i, _):
        share_copy(i, (dp + i) % dp_count, dp).start()
        return 0

    send(Z + 1, rows_of(z, gx, y), near_peer, own_piece)
    relay(Z + 2, rows_of(z, gx, y), across_peer, RELAY, own_piece)
    send(Y, rows_of(z, gx, y), y_peer, own_piece)
    send(CORE0, rows_of(z, 0, y, count=shard), other_core, w_hbm)

    lax.fori_loop(1, dp_count, send_share, 0)
    held[pl.ds(dp * shrink.shape[0], shrink.shape[0])] = shares[dp]

    own_ids = pltpu.make_async_copy(request_ref, ids.at[gx], local_sem.at[2])
    own_ids.start()
    swap_ids.wait_recv()
    their_ids = pltpu.make_async_copy(ids_in, ids.at[fx], local_sem.at[3])
    their_ids.start()
    own_ids.wait()
    their_ids.wait()

    def pass_first():
        landed(Y, rows_of(z, gx, fy))
        send(DX0, rows_of(z, gx, fy), x_peer)
        send(CY, rows_of(z, gx, fy), other_core)

    def pass_layer(i):
        rows = rows_of(layers[i], gx, y)
        landed(Z + i, rows)
        relay((Z + 3, Z + 2, Z + 3)[i - 1], rows, across_peer if i == 1 else near_peer, RELAY + i)
        send(Y + i, rows, y_peer)
        send(X + i, rows, x_peer)
        send(CZ + i, rows, other_core)

    def pass_sides(i):
        rows = rows_of(layers[i], fx, y)
        landed(X + i, rows)
        send(DY + i, rows_of(layers[i], fx, y, 0, half), y_peer)
        send(CX + i, rows, other_core)
        rows = rows_of(layers[i], gx, fy)
        landed(Y + i, rows)
        send(DX + i, rows_of(layers[i], gx, fy, half, half), x_peer)
        send(CY + i, rows, other_core)

    def pass_corner(i):
        if i == 0:
            landed(DX0, rows_of(z, fx, fy))
        else:
            landed(DY + i, rows_of(layers[i], fx, fy, 0, half))
            landed(DX + i, rows_of(layers[i], fx, fy, half, half))
        send(CD + i, rows_of(layers[i], fx, fy), other_core)

    def wait_share(i, _):
        share_copy(i, dp, (dp + dp_count - i) % dp_count).wait_recv()
        return 0


    def pick_copy(i, to, holder):
        return pltpu.make_async_remote_copy(
            src_ref=picks.at[to], dst_ref=mine.at[:, holder],
            send_sem=two_send.at[i], recv_sem=two_recv.at[i],
            device_id=(to // dp_count, to % dp_count), device_id_type=MESH,
        )

    def pick(to, j):
        return held[adapter_slot[ids[to // dp_count, 0, (to % dp_count) * own + j]]]

    def send_pick(i, _):
        to = (me + i) % devices
        for j in range(own):
            picks[to, j] = pick(to, j)
        pick_copy(i, to, me).start()
        return 0


    block = 4 * shard
    column = 256
    def multiply(i):
        layer = layers[i]
        if i == 0:
            landed(CORE0, rows_of_other(z, 0, y, count=shard))
        else:
            landed(CZ + i, rows_of_other(layer, gx, y))
            landed(CX + i, rows_of_other(layer, fx, y))
        landed(CY + i, rows_of_other(layer, gx, fy))
        landed(CD + i, rows_of_other(layer, fx, fy))
        place = pl.ds(pl.multiple_of(layer * block, block), block)

        def add(n, _):
            cols = pl.ds(pl.multiple_of(n * column, column), column)
            term = jnp.dot(tok[:, place], weight[place, cols], preferred_element_type=jnp.float32)
            total[:, cols] = term if i == 0 else total[:, cols] + term
            return 0

        lax.fori_loop(0, total.shape[1] // column, add, 0)

    pass_first()
    pass_layer(1)
    pass_layer(2)
    pass_sides(1)
    pass_layer(3)
    pass_sides(2)
    lax.fori_loop(1, dp_count, wait_share, 0)
    lax.fori_loop(1, devices, send_pick, 0)
    for j in range(own):
        mine[j, me] = pick(me, j)
    pass_sides(3)
    load_tok.wait()
    load_w.wait()
    pass_corner(0)
    pass_corner(1)
    multiply(0)
    pass_corner(2)
    multiply(1)
    pass_corner(3)
    multiply(2)
    multiply(3)
    seg = tok.shape[0] // own
    per_layer = dp_count // LAYERS
    shrunk = [jnp.zeros((seg, rank), jnp.float32) for _ in range(own)]
    for i in range(LAYERS):
        for g in range(groups):
            first = g * dp_count + layers[i] * per_layer

            def wait_pick(t, _):
                holder = first + t

                @pl.when(holder != me)
                def _():
                    pick_copy((me - holder + devices) % devices, me, holder).wait_recv()

                return 0

            lax.fori_loop(0, per_layer, wait_pick, 0)
            span = pl.ds(pl.multiple_of(first * LANES, LANES), per_layer * LANES)
            for j in range(own):
                down = jnp.concatenate([mine[j, first + t, :rank, :] for t in range(per_layer)], axis=1)
                shrunk[j] += lax.dot_general(
                    tok[pl.ds(j * seg, seg), span], down, (((1,), (1,)), ((), ())),
                    preferred_element_type=jnp.float32,
                )
    for j in range(own):
        lines = pl.ds(j * seg, seg)
        up = jnp.concatenate(
            [
                jnp.concatenate([mine[j, r * 8 + c, rank:, :] for c in range(8)], axis=1)
                for r in range(rank // TILE)
            ],
            axis=0,
        )
        low_rank = jnp.dot(
            shrunk[j].astype(jnp.bfloat16), up, preferred_element_type=jnp.float32
        ).astype(jnp.bfloat16)
        out_ref[lines, :] = (total[lines, :] + low_rank.astype(jnp.float32)).astype(out_ref.dtype)

    for copy in sent:
        copy.wait_send()

    @pl.when(inner == 1)
    def _():
        for copy in relays:
            copy.wait_send()

    swap_ids.wait_send()

    def drain_one(i, _):
        share_copy(i, (dp + i) % dp_count, dp).wait_send()
        return 0

    def drain_two(i, _):
        pick_copy(i, (me + i) % devices, me).wait_send()
        return 0

    lax.fori_loop(1, dp_count, drain_one, 0)
    lax.fori_loop(1, devices, drain_two, 0)


def in_one_kernel(tokens, base_weight, shrink_store, expand_store, request_adapter, adapter_slot):
    groups, dp_count = lax.axis_size("groups"), lax.axis_size("dp")
    devices = groups * dp_count
    rows, width = tokens.shape
    slots, _, rank = shrink_store.shape
    outs = base_weight.shape[1]
    requests = request_adapter.shape[0]
    own = requests // dp_count
    tall = rank + TILE
    bf16 = jnp.bfloat16
    vmem = pl.BlockSpec(memory_space=pltpu.VMEM)
    anywhere = pl.BlockSpec(memory_space=pl.ANY)
    dma = pltpu.SemaphoreType.DMA
    return pl.pallas_call(
        prefill_kernel,
        out_shape=jax.ShapeDtypeStruct((rows, outs), bf16),
        in_specs=[vmem, pl.BlockSpec(memory_space=pltpu.SMEM), anywhere, anywhere, vmem, vmem],
        out_specs=vmem,
        scratch_shapes=[
            pltpu.VMEM((width, outs), bf16),
            pltpu.VMEM((rows, width), bf16),
            pltpu.VMEM((rows, outs), jnp.float32),
            pltpu.VMEM((dp_count, slots, tall, LANES), bf16),
            pltpu.VMEM((dp_count * slots, tall, LANES), bf16),
            pltpu.VMEM((devices, own, tall, LANES), bf16),
            pltpu.VMEM((own, devices, tall, LANES), bf16),
            pltpu.VMEM((1, requests), jnp.int32),
            pltpu.SMEM((groups, 1, requests), jnp.int32),
            dma((4,)),
            dma((SENDS,)),
            dma((MESSAGES,)),
            dma((dp_count,)),
            dma((dp_count,)),
            dma((devices,)),
            dma((devices,)),
            dma,
            dma,
        ],
        compiler_params=pltpu.CompilerParams(
            collective_id=0, has_side_effects=True, vmem_limit_bytes=56 * 1024 * 1024
        ),
        cost_estimate=pl.CostEstimate(
            flops=2 * rows * width * (outs + 2 * rank), bytes_accessed=16 * 1024 * 1024, transcendentals=0
        ),
    )(request_adapter.reshape(1, requests), adapter_slot, tokens, base_weight,
      jnp.swapaxes(shrink_store, 1, 2), expand_store)


def routed_by_collectives(tokens, base_weight, shrink_store, expand_store, request_adapter, adapter_slot):
    dp_count = lax.axis_size("dp")
    slots, width, rank = shrink_store.shape
    outs = expand_store.shape[2]
    requests = request_adapter.shape[0]
    own = requests // dp_count
    gathered = lax.all_gather(base_weight, "dp", axis=0, tiled=True)
    slot_ids = adapter_slot[request_adapter]
    shares = jnp.concatenate(
        [
            shrink_store.reshape(slots, dp_count, -1),
            expand_store.reshape(slots, dp_count, -1),
        ],
        axis=2,
    )
    held = lax.all_to_all(shares, "dp", split_axis=1, concat_axis=0, tiled=True)
    picked = jnp.take(held, slot_ids, axis=0)
    mine = lax.all_to_all(picked, "dp", split_axis=0, concat_axis=1, tiled=True)
    cut = width * rank // dp_count
    down = mine[:, :, :cut].reshape(own, width, rank)
    up = mine[:, :, cut:].reshape(own, rank, outs)
    grouped = tokens.reshape(own, -1, width)
    shrunk = jnp.einsum("qsd,qdr->qsr", grouped, down, preferred_element_type=jnp.float32).astype(jnp.bfloat16)
    low_rank = jnp.einsum("qsr,qrc->qsc", shrunk, up, preferred_element_type=jnp.float32).astype(jnp.bfloat16)
    base_out = jnp.dot(tokens, gathered, preferred_element_type=jnp.float32)
    low_rank = low_rank.reshape(base_out.shape)
    return (base_out + low_rank.astype(jnp.float32)).astype(jnp.bfloat16)


def solution(mesh):
    square = mesh.shape["groups"] == 2 and mesh.shape["dp"] == 16
    return jax.shard_map(
        in_one_kernel if square else routed_by_collectives,
        mesh=mesh,
        in_specs=(
            P(("groups", "dp"), None),
            P("dp", None),
            P("dp", None, None),
            P("dp", None, None),
            P("groups"),
            P(),
        ),
        out_specs=P(("groups", "dp"), None),
        check_vma=False,
    )
```

```python
import jax
import jax.numpy as jnp
from jax import lax
from jax.experimental import pallas as pl
from jax.experimental.pallas import tpu as pltpu
from jax.sharding import PartitionSpec as P

MESH = pl.DeviceIdType.MESH
LANES = 128
TILE = 16
LAYERS = 4
CORE0, Z, Y, X, DY, DX, DX0, CZ, CY, CX, CD = 0, 0, 4, 7, 10, 13, 17, 17, 21, 24, 28
MESSAGES = 32
RELAY = 32
SENDS = 36


def prefill_kernel(
    request_ref, adapter_slot, tok_hbm, w_hbm, shrink_hbm, expand_hbm, out_ref,
    weight, tok, total, shrink, expand, shares, held, picks, mine, ids_in, ids,
    local_sem, base_send, base_recv, one_send, one_recv, two_send, two_recv, ids_send, ids_recv, joined,
):
    gx, dp = lax.axis_index("groups"), lax.axis_index("dp")
    groups, dp_count = lax.axis_size("groups"), lax.axis_size("dp")
    devices = groups * dp_count
    me = gx * dp_count + dp
    core = dp % 2
    y = (dp // 2) % 2
    z = dp // 4
    shard = w_hbm.shape[0]
    piece = shard // 2
    by_y = piece * 2 // 4
    by_x = piece - by_y
    width = tok_hbm.shape[1]
    rank = shrink.shape[1]
    own = mine.shape[0]
    side = z // 2
    inner = ((z + 1) // 2) % 2
    near, across = z + 1 - 2 * (z % 2), LAYERS - 1 - z
    layers = [z, near, 2 - side, 3 - 3 * side]

    barrier = pltpu.get_barrier_semaphore()

    near_peer = (gx, (near * 2 + y) * 2 + core)
    across_peer = (gx, (across * 2 + y) * 2 + core)
    other_core = (gx, dp + 1 - 2 * core)
    x_peer = (1 - gx, dp)
    y_peer = (gx, dp + 2 - 4 * y)
    peers = [other_core, y_peer, x_peer, near_peer, across_peer]
    for peer in peers:
        pl.semaphore_signal(barrier, inc=1, device_id=peer, device_id_type=MESH)
    load_shrink = pltpu.make_async_copy(shrink_hbm, shrink, local_sem.at[4])
    load_shrink.start()
    load_expand = pltpu.make_async_copy(expand_hbm, expand, local_sem.at[5])
    load_expand.start()
    load_tok = pltpu.make_async_copy(tok_hbm, tok, local_sem.at[0])
    load_tok.start()
    load_w = pltpu.make_async_copy(
        w_hbm, weight.at[pl.ds(pl.multiple_of(dp * shard, shard), shard)], local_sem.at[1]
    )
    load_w.start()

    share_first = gx * dp_count

    def pack(i, _):
        k = share_first + i
        col = pl.multiple_of(k * LANES, LANES)
        up_row = pl.multiple_of((k // 8) * TILE, TILE)
        up_col = pl.multiple_of((k % 8) * LANES, LANES)
        for s in range(shrink.shape[0]):
            shares[i, s, :rank, :] = shrink[s, :, pl.ds(col, LANES)]
            shares[i, s, rank:, :] = expand[s, pl.ds(up_row, TILE), pl.ds(up_col, LANES)]
        return 0

    pl.semaphore_wait(barrier, len(peers))

    def rows_of(layer, of_x, of_y, first=0, count=piece):
        owner = (layer * 2 + of_y) * 2 + core
        return pl.ds(pl.multiple_of(owner * shard + of_x * piece + first, TILE), count)

    def rows_of_other(layer, of_x, of_y, count=piece):
        owner = (layer * 2 + of_y) * 2 + 1 - core
        return pl.ds(pl.multiple_of(owner * shard + of_x * piece, TILE), count)

    def message(number, src, rows, target, send_number=None):
        return pltpu.make_async_remote_copy(
            src_ref=src, dst_ref=weight.at[rows],
            send_sem=base_send.at[number if send_number is None else send_number], recv_sem=base_recv.at[number],
            device_id=target, device_id_type=MESH,
        )

    sent = []

    def send(number, rows, target, src=None):
        copy = message(number, weight.at[rows] if src is None else src, rows, target)
        copy.start()
        sent.append(copy)

    def landed(number, rows):
        message(number, weight.at[rows], rows, other_core).wait_recv()

    fx, fy = 1 - gx, 1 - y
    other_core = (gx, dp + 1 - 2 * core)
    x_peer = (fx, dp)
    y_peer = (gx, dp + 2 - 4 * y)
    own_piece = w_hbm.at[pl.ds(pl.multiple_of(gx * piece, TILE), piece)]

    swap_ids = pltpu.make_async_remote_copy(
        src_ref=request_ref, dst_ref=ids_in, send_sem=ids_send, recv_sem=ids_recv,
        device_id=x_peer, device_id_type=MESH,
    )
    swap_ids.start()
    near_peer = (gx, (near * 2 + y) * 2 + core)
    across_peer = (gx, (across * 2 + y) * 2 + core)
    relays = []

    def relay(number, rows, target, send_number, src=None):
        copy = message(number, weight.at[rows] if src is None else src, rows, target, send_number)
        relays.append(copy)

        @pl.when(inner == 1)
        def _():
            copy.start()

    def share_copy(i, to, owner):
        return pltpu.make_async_remote_copy(
            src_ref=shares.at[to], dst_ref=held.at[pl.ds(owner * shrink.shape[0], shrink.shape[0])],
            send_sem=one_send.at[i], recv_sem=one_recv.at[i],
            device_id=(gx, to), device_id_type=MESH,
        )

    def send_share(i, _):
        share_copy(i, (dp + i) % dp_count, dp).start()
        return 0

    send(Z + 1, rows_of(z, gx, y), near_peer, own_piece)
    relay(Z + 2, rows_of(z, gx, y), across_peer, RELAY, own_piece)
    send(Y, rows_of(z, gx, y), y_peer, own_piece)
    send(CORE0, rows_of(z, 0, y, count=shard), other_core, w_hbm)

    pl.semaphore_signal(joined.at[0], inc=1, device_id=peers[0], device_id_type=MESH)
    load_shrink.wait()
    load_expand.wait()
    lax.fori_loop(0, dp_count, pack, 0)
    for r in range(len(peers)):
        if r > 0:
            pl.semaphore_signal(joined.at[r], inc=1, device_id=peers[r], device_id_type=MESH)
        pl.semaphore_wait(joined.at[r], 1)
    lax.fori_loop(1, dp_count, send_share, 0)
    held[pl.ds(dp * shrink.shape[0], shrink.shape[0])] = shares[dp]

    own_ids = pltpu.make_async_copy(request_ref, ids.at[gx], local_sem.at[2])
    own_ids.start()
    swap_ids.wait_recv()
    their_ids = pltpu.make_async_copy(ids_in, ids.at[fx], local_sem.at[3])
    their_ids.start()
    own_ids.wait()
    their_ids.wait()

    def pass_first():
        landed(Y, rows_of(z, gx, fy))
        send(DX0, rows_of(z, gx, fy), x_peer)
        send(CY, rows_of(z, gx, fy), other_core)

    def pass_layer(i):
        rows = rows_of(layers[i], gx, y)
        landed(Z + i, rows)
        relay((Z + 3, Z + 2, Z + 3)[i - 1], rows, across_peer if i == 1 else near_peer, RELAY + i)
        send(Y + i, rows, y_peer)
        send(X + i, rows, x_peer)
        send(CZ + i, rows, other_core)

    def pass_sides(i):
        rows = rows_of(layers[i], fx, y)
        landed(X + i, rows)
        send(DY + i, rows_of(layers[i], fx, y, 0, by_y), y_peer)
        send(CX + i, rows, other_core)
        rows = rows_of(layers[i], gx, fy)
        landed(Y + i, rows)
        send(DX + i, rows_of(layers[i], gx, fy, by_y, by_x), x_peer)
        send(CY + i, rows, other_core)

    def pass_corner(i):
        if i == 0:
            landed(DX0, rows_of(z, fx, fy))
        else:
            landed(DY + i, rows_of(layers[i], fx, fy, 0, by_y))
            landed(DX + i, rows_of(layers[i], fx, fy, by_y, by_x))
        send(CD + i, rows_of(layers[i], fx, fy), other_core)

    def wait_share(i, _):
        share_copy(i, dp, (dp + dp_count - i) % dp_count).wait_recv()
        return 0


    def pick_copy(i, to, holder):
        return pltpu.make_async_remote_copy(
            src_ref=picks.at[to], dst_ref=mine.at[:, holder],
            send_sem=two_send.at[i], recv_sem=two_recv.at[i],
            device_id=(to // dp_count, to % dp_count), device_id_type=MESH,
        )

    def pick(to, j):
        return held[adapter_slot[ids[to // dp_count, 0, (to % dp_count) * own + j]]]

    members = dp_count // 2
    seat = dp % members

    def partner(i, way):
        of_side = (side + 1 + i // dp_count) % 2
        return ((gx + i // members) % groups) * dp_count + of_side * members + (seat + way * i + dp_count * 2) % members

    def turn_of(holder):
        same = 1 - (holder // members + side) % 2
        away = (holder // dp_count + gx) % 2
        return same * dp_count + away * members + (seat + members - holder % members) % members

    def send_pick(i, _):
        to = partner(i, 1)
        for j in range(own):
            picks[to, j] = pick(to, j)
        pick_copy(i, to, me).start()
        return 0


    block = 4 * shard
    column = 256
    def multiply(i):
        layer = layers[i]
        if i == 0:
            landed(CORE0, rows_of_other(z, 0, y, count=shard))
        else:
            landed(CZ + i, rows_of_other(layer, gx, y))
            landed(CX + i, rows_of_other(layer, fx, y))
        landed(CY + i, rows_of_other(layer, gx, fy))
        landed(CD + i, rows_of_other(layer, fx, fy))
        place = pl.ds(pl.multiple_of(layer * block, block), block)

        def add(n, _):
            cols = pl.ds(pl.multiple_of(n * column, column), column)
            term = jnp.dot(tok[:, place], weight[place, cols], preferred_element_type=jnp.float32)
            total[:, cols] = term if i == 0 else total[:, cols] + term
            return 0

        lax.fori_loop(0, total.shape[1] // column, add, 0)

    pass_first()
    pass_layer(1)
    pass_layer(2)
    pass_sides(1)
    pass_layer(3)
    pass_sides(2)
    lax.fori_loop(1, dp_count, wait_share, 0)
    lax.fori_loop(0, dp_count, send_pick, 0)
    pass_sides(3)
    load_tok.wait()
    load_w.wait()
    pass_corner(0)
    lax.fori_loop(dp_count + 1, devices, send_pick, 0)
    for j in range(own):
        mine[j, me] = pick(me, j)
    pass_corner(1)
    multiply(0)
    pass_corner(2)
    multiply(1)
    pass_corner(3)
    multiply(2)
    multiply(3)
    seg = tok.shape[0] // own
    per_layer = dp_count // LAYERS
    shrunk = [jnp.zeros((seg, rank), jnp.float32) for _ in range(own)]
    for i in range(LAYERS):
        for g in range(groups):
            first = g * dp_count + layers[i] * per_layer

            def wait_pick(t, _):
                holder = first + t

                @pl.when(holder != me)
                def _():
                    pick_copy(turn_of(holder), me, holder).wait_recv()

                return 0

            lax.fori_loop(0, per_layer, wait_pick, 0)
            span = pl.ds(pl.multiple_of(first * LANES, LANES), per_layer * LANES)
            for j in range(own):
                down = jnp.concatenate([mine[j, first + t, :rank, :] for t in range(per_layer)], axis=1)
                shrunk[j] += lax.dot_general(
                    tok[pl.ds(j * seg, seg), span], down, (((1,), (1,)), ((), ())),
                    preferred_element_type=jnp.float32,
                )
    for j in range(own):
        lines = pl.ds(j * seg, seg)
        up = jnp.concatenate(
            [
                jnp.concatenate([mine[j, r * 8 + c, rank:, :] for c in range(8)], axis=1)
                for r in range(rank // TILE)
            ],
            axis=0,
        )
        low_rank = jnp.dot(
            shrunk[j].astype(jnp.bfloat16), up, preferred_element_type=jnp.float32
        ).astype(jnp.bfloat16)
        out_ref[lines, :] = (total[lines, :] + low_rank.astype(jnp.float32)).astype(out_ref.dtype)

    for copy in sent:
        copy.wait_send()

    @pl.when(inner == 1)
    def _():
        for copy in relays:
            copy.wait_send()

    swap_ids.wait_send()

    def drain_one(i, _):
        share_copy(i, (dp + i) % dp_count, dp).wait_send()
        return 0

    def drain_two(i, _):
        pick_copy(i, partner(i, 1), me).wait_send()
        return 0

    lax.fori_loop(1, dp_count, drain_one, 0)
    lax.fori_loop(0, dp_count, drain_two, 0)
    lax.fori_loop(dp_count + 1, devices, drain_two, 0)


def in_one_kernel(tokens, base_weight, shrink_store, expand_store, request_adapter, adapter_slot):
    groups, dp_count = lax.axis_size("groups"), lax.axis_size("dp")
    devices = groups * dp_count
    rows, width = tokens.shape
    slots, _, rank = shrink_store.shape
    outs = base_weight.shape[1]
    requests = request_adapter.shape[0]
    own = requests // dp_count
    tall = rank + TILE
    bf16 = jnp.bfloat16
    vmem = pl.BlockSpec(memory_space=pltpu.VMEM)
    anywhere = pl.BlockSpec(memory_space=pl.ANY)
    dma = pltpu.SemaphoreType.DMA
    return pl.pallas_call(
        prefill_kernel,
        out_shape=jax.ShapeDtypeStruct((rows, outs), bf16),
        in_specs=[vmem, pl.BlockSpec(memory_space=pltpu.SMEM), anywhere, anywhere, anywhere, anywhere],
        out_specs=vmem,
        scratch_shapes=[
            pltpu.VMEM((width, outs), bf16),
            pltpu.VMEM((rows, width), bf16),
            pltpu.VMEM((rows, outs), jnp.float32),
            pltpu.VMEM((slots, rank, width), bf16),
            pltpu.VMEM((slots, rank, outs), bf16),
            pltpu.VMEM((dp_count, slots, tall, LANES), bf16),
            pltpu.VMEM((dp_count * slots, tall, LANES), bf16),
            pltpu.VMEM((devices, own, tall, LANES), bf16),
            pltpu.VMEM((own, devices, tall, LANES), bf16),
            pltpu.VMEM((1, requests), jnp.int32),
            pltpu.SMEM((groups, 1, requests), jnp.int32),
            dma((6,)),
            dma((SENDS,)),
            dma((MESSAGES,)),
            dma((dp_count,)),
            dma((dp_count,)),
            dma((devices,)),
            dma((devices,)),
            dma,
            dma,
            pltpu.SemaphoreType.REGULAR((5,)),
        ],
        compiler_params=pltpu.CompilerParams(
            collective_id=0, has_side_effects=True, vmem_limit_bytes=56 * 1024 * 1024
        ),
        cost_estimate=pl.CostEstimate(
            flops=2 * rows * width * (outs + 2 * rank), bytes_accessed=16 * 1024 * 1024, transcendentals=0
        ),
    )(request_adapter.reshape(1, requests), adapter_slot, tokens, base_weight,
      jnp.swapaxes(shrink_store, 1, 2), expand_store)


def routed_by_collectives(tokens, base_weight, shrink_store, expand_store, request_adapter, adapter_slot):
    dp_count = lax.axis_size("dp")
    slots, width, rank = shrink_store.shape
    outs = expand_store.shape[2]
    requests = request_adapter.shape[0]
    own = requests // dp_count
    gathered = lax.all_gather(base_weight, "dp", axis=0, tiled=True)
    slot_ids = adapter_slot[request_adapter]
    shares = jnp.concatenate(
        [
            shrink_store.reshape(slots, dp_count, -1),
            expand_store.reshape(slots, dp_count, -1),
        ],
        axis=2,
    )
    held = lax.all_to_all(shares, "dp", split_axis=1, concat_axis=0, tiled=True)
    picked = jnp.take(held, slot_ids, axis=0)
    mine = lax.all_to_all(picked, "dp", split_axis=0, concat_axis=1, tiled=True)
    cut = width * rank // dp_count
    down = mine[:, :, :cut].reshape(own, width, rank)
    up = mine[:, :, cut:].reshape(own, rank, outs)
    grouped = tokens.reshape(own, -1, width)
    shrunk = jnp.einsum("qsd,qdr->qsr", grouped, down, preferred_element_type=jnp.float32).astype(jnp.bfloat16)
    low_rank = jnp.einsum("qsr,qrc->qsc", shrunk, up, preferred_element_type=jnp.float32).astype(jnp.bfloat16)
    base_out = jnp.dot(tokens, gathered, preferred_element_type=jnp.float32)
    low_rank = low_rank.reshape(base_out.shape)
    return (base_out + low_rank.astype(jnp.float32)).astype(jnp.bfloat16)


def solution(mesh):
    square = mesh.shape["groups"] == 2 and mesh.shape["dp"] == 16
    return jax.shard_map(
        in_one_kernel if square else routed_by_collectives,
        mesh=mesh,
        in_specs=(
            P(("groups", "dp"), None),
            P("dp", None),
            P("dp", None, None),
            P("dp", None, None),
            P("groups"),
            P(),
        ),
        out_specs=P(("groups", "dp"), None),
        check_vma=False,
    )
```

```python
import jax
import jax.numpy as jnp
from jax import lax
from jax.experimental import pallas as pl
from jax.experimental.pallas import tpu as pltpu
from jax.sharding import PartitionSpec as P

MESH = pl.DeviceIdType.MESH
LANES = 128
TILE = 16
LAYERS = 4
CORE0, Z, Y, X, DY, DX, DX0, CZ, CY, CX, CD = 0, 0, 4, 7, 10, 13, 17, 17, 21, 24, 28
MESSAGES = 32
RELAY = 32
SENDS = 36


def prefill_kernel(
    request_ref, adapter_slot, tok_hbm, w_hbm, shrink_hbm, expand_hbm, out_ref,
    weight, tok, total, shrink, expand, shares, held, picks, mine, ids_in, ids,
    local_sem, base_send, base_recv, one_send, one_recv, two_send, two_recv, ids_send, ids_recv, joined,
):
    gx, dp = lax.axis_index("groups"), lax.axis_index("dp")
    groups, dp_count = lax.axis_size("groups"), lax.axis_size("dp")
    devices = groups * dp_count
    me = gx * dp_count + dp
    core = dp % 2
    y = (dp // 2) % 2
    z = dp // 4
    shard = w_hbm.shape[0]
    piece = shard // 2
    by_y = piece * 2 // 4
    by_x = piece - by_y
    width = tok_hbm.shape[1]
    rank = shrink.shape[1]
    own = mine.shape[0]
    side = z // 2
    inner = ((z + 1) // 2) % 2
    near, across = z + 1 - 2 * (z % 2), LAYERS - 1 - z
    layers = [z, near, 2 - side, 3 - 3 * side]

    barrier = pltpu.get_barrier_semaphore()

    near_peer = (gx, (near * 2 + y) * 2 + core)
    across_peer = (gx, (across * 2 + y) * 2 + core)
    other_core = (gx, dp + 1 - 2 * core)
    x_peer = (1 - gx, dp)
    y_peer = (gx, dp + 2 - 4 * y)
    peers = [other_core, y_peer, x_peer, near_peer, across_peer]
    for peer in peers:
        pl.semaphore_signal(barrier, inc=1, device_id=peer, device_id_type=MESH)
    load_shrink = pltpu.make_async_copy(shrink_hbm, shrink, local_sem.at[4])
    load_shrink.start()
    load_expand = pltpu.make_async_copy(expand_hbm, expand, local_sem.at[5])
    load_expand.start()
    load_tok = pltpu.make_async_copy(tok_hbm, tok, local_sem.at[0])
    load_tok.start()
    load_w = pltpu.make_async_copy(
        w_hbm, weight.at[pl.ds(pl.multiple_of(dp * shard, shard), shard)], local_sem.at[1]
    )
    load_w.start()

    share_first = gx * dp_count

    def pack(i, _):
        k = share_first + i
        col = pl.multiple_of(k * LANES, LANES)
        up_row = pl.multiple_of((k // 8) * TILE, TILE)
        up_col = pl.multiple_of((k % 8) * LANES, LANES)
        for s in range(shrink.shape[0]):
            shares[i, s, :rank, :] = shrink[s, :, pl.ds(col, LANES)]
            shares[i, s, rank:, :] = expand[s, pl.ds(up_row, TILE), pl.ds(up_col, LANES)]
        return 0

    pl.semaphore_wait(barrier, len(peers))

    def rows_of(layer, of_x, of_y, first=0, count=piece):
        owner = (layer * 2 + of_y) * 2 + core
        return pl.ds(pl.multiple_of(owner * shard + of_x * piece + first, TILE), count)

    def rows_of_other(layer, of_x, of_y, count=piece):
        owner = (layer * 2 + of_y) * 2 + 1 - core
        return pl.ds(pl.multiple_of(owner * shard + of_x * piece, TILE), count)

    def message(number, src, rows, target, send_number=None):
        return pltpu.make_async_remote_copy(
            src_ref=src, dst_ref=weight.at[rows],
            send_sem=base_send.at[number if send_number is None else send_number], recv_sem=base_recv.at[number],
            device_id=target, device_id_type=MESH,
        )

    sent = []

    def send(number, rows, target, src=None):
        copy = message(number, weight.at[rows] if src is None else src, rows, target)
        copy.start()
        sent.append(copy)

    def landed(number, rows):
        message(number, weight.at[rows], rows, other_core).wait_recv()

    fx, fy = 1 - gx, 1 - y
    other_core = (gx, dp + 1 - 2 * core)
    x_peer = (fx, dp)
    y_peer = (gx, dp + 2 - 4 * y)
    own_piece = w_hbm.at[pl.ds(pl.multiple_of(gx * piece, TILE), piece)]

    swap_ids = pltpu.make_async_remote_copy(
        src_ref=request_ref, dst_ref=ids_in, send_sem=ids_send, recv_sem=ids_recv,
        device_id=x_peer, device_id_type=MESH,
    )
    swap_ids.start()
    near_peer = (gx, (near * 2 + y) * 2 + core)
    across_peer = (gx, (across * 2 + y) * 2 + core)
    relays = []

    def relay(number, rows, target, send_number, src=None):
        copy = message(number, weight.at[rows] if src is None else src, rows, target, send_number)
        relays.append(copy)

        @pl.when(inner == 1)
        def _():
            copy.start()

    def share_copy(i, to, owner):
        return pltpu.make_async_remote_copy(
            src_ref=shares.at[to], dst_ref=held.at[pl.ds(owner * shrink.shape[0], shrink.shape[0])],
            send_sem=one_send.at[i], recv_sem=one_recv.at[i],
            device_id=(gx, to), device_id_type=MESH,
        )

    def send_share(i, _):
        share_copy(i, (dp + i) % dp_count, dp).start()
        return 0

    send(Z + 1, rows_of(z, gx, y), near_peer, own_piece)
    relay(Z + 2, rows_of(z, gx, y), across_peer, RELAY, own_piece)
    send(Y, rows_of(z, gx, y), y_peer, own_piece)
    send(CORE0, rows_of(z, 0, y, count=shard), other_core, w_hbm)

    pl.semaphore_signal(joined.at[0], inc=1, device_id=peers[0], device_id_type=MESH)
    load_shrink.wait()
    load_expand.wait()
    lax.fori_loop(0, dp_count, pack, 0)
    for r in range(len(peers)):
        if r > 0:
            pl.semaphore_signal(joined.at[r], inc=1, device_id=peers[r], device_id_type=MESH)
        pl.semaphore_wait(joined.at[r], 1)
    lax.fori_loop(1, dp_count, send_share, 0)
    held[pl.ds(dp * shrink.shape[0], shrink.shape[0])] = shares[dp]

    own_ids = pltpu.make_async_copy(request_ref, ids.at[gx], local_sem.at[2])
    own_ids.start()
    swap_ids.wait_recv()
    their_ids = pltpu.make_async_copy(ids_in, ids.at[fx], local_sem.at[3])
    their_ids.start()
    own_ids.wait()
    their_ids.wait()

    def pass_first():
        landed(Y, rows_of(z, gx, fy))
        send(DX0, rows_of(z, gx, fy), x_peer)
        send(CY, rows_of(z, gx, fy), other_core)

    def pass_layer(i):
        rows = rows_of(layers[i], gx, y)
        landed(Z + i, rows)
        relay((Z + 3, Z + 2, Z + 3)[i - 1], rows, across_peer if i == 1 else near_peer, RELAY + i)
        send(Y + i, rows, y_peer)
        send(X + i, rows, x_peer)
        send(CZ + i, rows, other_core)

    def pass_sides(i):
        rows = rows_of(layers[i], fx, y)
        landed(X + i, rows)
        send(DY + i, rows_of(layers[i], fx, y, 0, by_y), y_peer)
        send(CX + i, rows, other_core)
        rows = rows_of(layers[i], gx, fy)
        landed(Y + i, rows)
        send(DX + i, rows_of(layers[i], gx, fy, by_y, by_x), x_peer)
        send(CY + i, rows, other_core)

    def pass_corner(i):
        if i == 0:
            landed(DX0, rows_of(z, fx, fy))
        else:
            landed(DY + i, rows_of(layers[i], fx, fy, 0, by_y))
            landed(DX + i, rows_of(layers[i], fx, fy, by_y, by_x))
        send(CD + i, rows_of(layers[i], fx, fy), other_core)

    def wait_share(i, _):
        share_copy(i, dp, (dp + dp_count - i) % dp_count).wait_recv()
        return 0


    def pick_copy(i, to, holder):
        return pltpu.make_async_remote_copy(
            src_ref=picks.at[to], dst_ref=mine.at[:, holder],
            send_sem=two_send.at[i], recv_sem=two_recv.at[i],
            device_id=(to // dp_count, to % dp_count), device_id_type=MESH,
        )

    def pick(to, j):
        return held[adapter_slot[ids[to // dp_count, 0, (to % dp_count) * own + j]]]

    members = dp_count // 2
    seat = dp % members

    def partner(i, way):
        of_side = (side + 1 + i // dp_count) % 2
        return ((gx + i // members) % groups) * dp_count + of_side * members + (seat + way * i + dp_count * 2) % members

    def turn_of(holder):
        same = 1 - (holder // members + side) % 2
        away = (holder // dp_count + gx) % 2
        return same * dp_count + away * members + (seat + members - holder % members) % members

    def send_pick(i, _):
        to = partner(i, 1)
        for j in range(own):
            picks[to, j] = pick(to, j)
        pick_copy(i, to, me).start()
        return 0


    block = 4 * shard
    column = 256
    def multiply(i):
        layer = layers[i]
        if i == 0:
            landed(CORE0, rows_of_other(z, 0, y, count=shard))
        else:
            landed(CZ + i, rows_of_other(layer, gx, y))
            landed(CX + i, rows_of_other(layer, fx, y))
        landed(CY + i, rows_of_other(layer, gx, fy))
        landed(CD + i, rows_of_other(layer, fx, fy))
        place = pl.ds(pl.multiple_of(layer * block, block), block)

        def add(n, _):
            cols = pl.ds(pl.multiple_of(n * column, column), column)
            term = jnp.dot(tok[:, place], weight[place, cols], preferred_element_type=jnp.float32)
            total[:, cols] = term if i == 0 else total[:, cols] + term
            return 0

        lax.fori_loop(0, total.shape[1] // column, add, 0)

    pass_first()
    pass_layer(1)
    pass_layer(2)
    pass_sides(1)
    pass_layer(3)
    pass_sides(2)
    pass_sides(3)
    lax.fori_loop(1, dp_count, wait_share, 0)
    lax.fori_loop(0, dp_count, send_pick, 0)
    load_tok.wait()
    load_w.wait()
    pass_corner(0)
    pass_corner(1)
    lax.fori_loop(dp_count + 1, devices, send_pick, 0)
    for j in range(own):
        mine[j, me] = pick(me, j)
    multiply(0)
    pass_corner(2)
    multiply(1)
    pass_corner(3)
    multiply(2)
    multiply(3)
    seg = tok.shape[0] // own
    per_layer = dp_count // LAYERS
    shrunk = [jnp.zeros((seg, rank), jnp.float32) for _ in range(own)]
    for i in range(LAYERS):
        for g in range(groups):
            first = g * dp_count + layers[i] * per_layer

            def wait_pick(t, _):
                holder = first + t

                @pl.when(holder != me)
                def _():
                    pick_copy(turn_of(holder), me, holder).wait_recv()

                return 0

            lax.fori_loop(0, per_layer, wait_pick, 0)
            span = pl.ds(pl.multiple_of(first * LANES, LANES), per_layer * LANES)
            for j in range(own):
                down = jnp.concatenate([mine[j, first + t, :rank, :] for t in range(per_layer)], axis=1)
                shrunk[j] += lax.dot_general(
                    tok[pl.ds(j * seg, seg), span], down, (((1,), (1,)), ((), ())),
                    preferred_element_type=jnp.float32,
                )
    for j in range(own):
        lines = pl.ds(j * seg, seg)
        up = jnp.concatenate(
            [
                jnp.concatenate([mine[j, r * 8 + c, rank:, :] for c in range(8)], axis=1)
                for r in range(rank // TILE)
            ],
            axis=0,
        )
        low_rank = jnp.dot(
            shrunk[j].astype(jnp.bfloat16), up, preferred_element_type=jnp.float32
        ).astype(jnp.bfloat16)
        out_ref[lines, :] = (total[lines, :] + low_rank.astype(jnp.float32)).astype(out_ref.dtype)

    for copy in sent:
        copy.wait_send()

    @pl.when(inner == 1)
    def _():
        for copy in relays:
            copy.wait_send()

    swap_ids.wait_send()

    def drain_one(i, _):
        share_copy(i, (dp + i) % dp_count, dp).wait_send()
        return 0

    def drain_two(i, _):
        pick_copy(i, partner(i, 1), me).wait_send()
        return 0

    lax.fori_loop(1, dp_count, drain_one, 0)
    lax.fori_loop(0, dp_count, drain_two, 0)
    lax.fori_loop(dp_count + 1, devices, drain_two, 0)


def in_one_kernel(tokens, base_weight, shrink_store, expand_store, request_adapter, adapter_slot):
    groups, dp_count = lax.axis_size("groups"), lax.axis_size("dp")
    devices = groups * dp_count
    rows, width = tokens.shape
    slots, _, rank = shrink_store.shape
    outs = base_weight.shape[1]
    requests = request_adapter.shape[0]
    own = requests // dp_count
    tall = rank + TILE
    bf16 = jnp.bfloat16
    vmem = pl.BlockSpec(memory_space=pltpu.VMEM)
    anywhere = pl.BlockSpec(memory_space=pl.ANY)
    dma = pltpu.SemaphoreType.DMA
    return pl.pallas_call(
        prefill_kernel,
        out_shape=jax.ShapeDtypeStruct((rows, outs), bf16),
        in_specs=[vmem, pl.BlockSpec(memory_space=pltpu.SMEM), anywhere, anywhere, anywhere, anywhere],
        out_specs=vmem,
        scratch_shapes=[
            pltpu.VMEM((width, outs), bf16),
            pltpu.VMEM((rows, width), bf16),
            pltpu.VMEM((rows, outs), jnp.float32),
            pltpu.VMEM((slots, rank, width), bf16),
            pltpu.VMEM((slots, rank, outs), bf16),
            pltpu.VMEM((dp_count, slots, tall, LANES), bf16),
            pltpu.VMEM((dp_count * slots, tall, LANES), bf16),
            pltpu.VMEM((devices, own, tall, LANES), bf16),
            pltpu.VMEM((own, devices, tall, LANES), bf16),
            pltpu.VMEM((1, requests), jnp.int32),
            pltpu.SMEM((groups, 1, requests), jnp.int32),
            dma((6,)),
            dma((SENDS,)),
            dma((MESSAGES,)),
            dma((dp_count,)),
            dma((dp_count,)),
            dma((devices,)),
            dma((devices,)),
            dma,
            dma,
            pltpu.SemaphoreType.REGULAR((5,)),
        ],
        compiler_params=pltpu.CompilerParams(
            collective_id=0, has_side_effects=True, vmem_limit_bytes=56 * 1024 * 1024
        ),
        cost_estimate=pl.CostEstimate(
            flops=2 * rows * width * (outs + 2 * rank), bytes_accessed=16 * 1024 * 1024, transcendentals=0
        ),
    )(request_adapter.reshape(1, requests), adapter_slot, tokens, base_weight,
      jnp.swapaxes(shrink_store, 1, 2), expand_store)


def routed_by_collectives(tokens, base_weight, shrink_store, expand_store, request_adapter, adapter_slot):
    dp_count = lax.axis_size("dp")
    slots, width, rank = shrink_store.shape
    outs = expand_store.shape[2]
    requests = request_adapter.shape[0]
    own = requests // dp_count
    gathered = lax.all_gather(base_weight, "dp", axis=0, tiled=True)
    slot_ids = adapter_slot[request_adapter]
    shares = jnp.concatenate(
        [
            shrink_store.reshape(slots, dp_count, -1),
            expand_store.reshape(slots, dp_count, -1),
        ],
        axis=2,
    )
    held = lax.all_to_all(shares, "dp", split_axis=1, concat_axis=0, tiled=True)
    picked = jnp.take(held, slot_ids, axis=0)
    mine = lax.all_to_all(picked, "dp", split_axis=0, concat_axis=1, tiled=True)
    cut = width * rank // dp_count
    down = mine[:, :, :cut].reshape(own, width, rank)
    up = mine[:, :, cut:].reshape(own, rank, outs)
    grouped = tokens.reshape(own, -1, width)
    shrunk = jnp.einsum("qsd,qdr->qsr", grouped, down, preferred_element_type=jnp.float32).astype(jnp.bfloat16)
    low_rank = jnp.einsum("qsr,qrc->qsc", shrunk, up, preferred_element_type=jnp.float32).astype(jnp.bfloat16)
    base_out = jnp.dot(tokens, gathered, preferred_element_type=jnp.float32)
    low_rank = low_rank.reshape(base_out.shape)
    return (base_out + low_rank.astype(jnp.float32)).astype(jnp.bfloat16)


def solution(mesh):
    square = mesh.shape["groups"] == 2 and mesh.shape["dp"] == 16
    return jax.shard_map(
        in_one_kernel if square else routed_by_collectives,
        mesh=mesh,
        in_specs=(
            P(("groups", "dp"), None),
            P("dp", None),
            P("dp", None, None),
            P("dp", None, None),
            P("groups"),
            P(),
        ),
        out_specs=P(("groups", "dp"), None),
        check_vma=False,
    )
```
